256 devices in a mesh: row: 64 (over x, z, core), col: 4 (over y).
Axes of the slice: x: 4, y: 4, z: 8, core: 2. Of those that a mesh axis runs over, the one named last changes fastest.
Arguments:
- factor: bfloat16 [64, 16, 4, 256, 256], P('row', None, 'col'), may hold values from -0.09375 to 0.09375
- diag_inverse: bfloat16 [64, 256, 256], P('row'), may hold values from -2 to 2, as said below
- right_side: bfloat16 [64, 64, 256], P('row'), may hold values from -6 to 6
- levels: int32 [64], replicated, may hold values from 0 to 3
- pattern: int32 [64, 16, 4], P('row', None, 'col'), may hold values 0 or 1
Outputs:
- forward: bfloat16 [64, 64, 256], P('row')
- solution: bfloat16 [64, 64, 256], P('row')
The draws below stay inside these ranges and needn't reach their ends.
Inputs may be any that keep to these rules, and one draw needn't show every extreme that they name: `diag_inverse`: each block is the inverse of a factor diagonal block, nonsingular.
All inputs are finite; a program needn't handle non-finite values. No bound on the sum of `pattern` on one device may be relied on, other than what follows from the above.
Results may differ from the reference program's by a relative error of at most 0.014.
Values may be sent and summed in bfloat16 or wider, within the bound.
No kernel may reach another device: no remote copies, remote signals or barrier semaphores. Data moves between devices by JAX's collectives and lax.ppermute only.
A program may use at most 64 MiB of HBM per device.

```python
import math
import jax
import jax.numpy as jnp
from jax import lax

B = 256
NRHS = 64
LEVELS = 4
NB = 64
CPD = 16
N_COL = 4


def draw_diag_inverse(key, part):
    key = jax.random.fold_in(key, 1)
    scale_key, off_key = jax.random.split(key)
    scales = jax.random.uniform(scale_key, (NB, B), jnp.float32, 0.7, 1.3)
    spread = 0.5 / math.sqrt(B)
    offdiag = spread * jax.random.normal(off_key, (NB, B, B), jnp.float32)
    identity = jnp.eye(B, dtype=jnp.float32)
    return (identity[None] * scales[:, :, None] + offdiag).astype(jnp.bfloat16)


def with_ends(drawn, key, smallest, top_value):
    extent = drawn.shape
    spot = [jax.random.randint(jax.random.fold_in(key, axis), (), 0, extent[axis]) for axis in range(len(extent))]
    drawn = drawn.at[tuple(spot)].set(smallest)
    longest = extent.index(max(extent))
    spot[longest] = (spot[longest] + 1) % extent[longest]
    return drawn.at[tuple(spot)].set(top_value)


def steps_of(own_key, extent, pieces, low, largest):
    factor_of, own = 1.0, jax.random.fold_in(own_key, 6)
    for position, shards_of in pieces:
        draws = jnp.exp(jax.random.uniform(jax.random.fold_in(own, position), (shards_of,), jnp.float32, low / len(pieces), largest / len(pieces)))
        factor_of = factor_of * jnp.repeat(draws, extent[position] // shards_of).reshape([-1 if axis == position else 1 for axis in range(len(extent))])
    return factor_of


def noise(own_key, extent, scale, limit, pieces=(), kind=jnp.bfloat16):
    drawn = scale * jax.random.normal(own_key, extent, jnp.float32)
    if pieces:
        drawn = drawn * steps_of(own_key, extent, pieces, -0.22, 0.18)
    return jnp.clip(drawn, -limit, limit).astype(kind)


def setup_inputs(seed: int = 0) -> dict:
    streams_of = jax.random.split(jax.random.key(seed), 6)
    factor = noise(streams_of[0], (NB, CPD, N_COL, B, B), (B * NB // 4) ** -0.5, 0.09375, ((0, 64), (2, 4)))
    diag_inverse = draw_diag_inverse(jax.random.fold_in(streams_of[5], 71), 0)
    right_side = noise(streams_of[2], (NB, NRHS, B), 1.0, 6.0, ((0, 64),))
    levels = with_ends(jax.random.randint(streams_of[3], (NB,), 0, LEVELS), jax.random.fold_in(streams_of[3], 1), 0, LEVELS - 1).astype(jnp.int32)
    pattern = with_ends((jax.random.randint(streams_of[4], (NB, CPD, N_COL), 0, 2) < 1).astype(jnp.int32), jax.random.fold_in(streams_of[4], 1), 0, 1)
    return dict(factor=factor, diag_inverse=diag_inverse, right_side=right_side, levels=levels, pattern=pattern)


def reference(factor, diag_inverse, right_side, levels, pattern):
    blocks = factor.reshape(NB, NB, B, B)
    pattern_full = pattern.reshape(NB, NB)
    usable = ((pattern_full == 1) & (levels[None, :] < levels[:, None])).astype(jnp.float32)
    inverse_f = diag_inverse.astype(jnp.float32)
    solved = jnp.zeros((NB, NRHS, B), jnp.bfloat16)
    for level in range(LEVELS):
        solved_f = solved.astype(jnp.float32)

        def row_sum(items):
            block_row, use_row = items
            masked = solved_f * use_row[:, None, None]
            return jnp.einsum("jab,jkb->ka", block_row.astype(jnp.float32), masked)

        sums = lax.map(row_sum, (blocks, usable))
        shifted = (right_side.astype(jnp.float32) - sums).astype(jnp.bfloat16)
        fresh_rows = jnp.einsum("ikb,iab->ika", shifted.astype(jnp.float32), inverse_f).astype(jnp.bfloat16)
        solved = jnp.where((levels == level)[:, None, None], fresh_rows, solved)
    forward = solved
    result = jnp.zeros((NB, NRHS, B), jnp.bfloat16)
    for level in range(LEVELS - 1, -1, -1):
        result_f = result.astype(jnp.float32)

        def add_row(carry, items):
            block_row, use_row, result_row = items
            term = jnp.einsum("jab,ka->jkb", block_row.astype(jnp.float32), result_row)
            return carry + term * use_row[:, None, None], None

        sums, unused = lax.scan(add_row, jnp.zeros((NB, NRHS, B), jnp.float32), (blocks, usable, result_f))
        shifted = (forward.astype(jnp.float32) - sums).astype(jnp.bfloat16)
        fresh_rows = jnp.einsum("ika,iab->ikb", shifted.astype(jnp.float32), inverse_f).astype(jnp.bfloat16)
        result = jnp.where((levels == level)[:, None, None], fresh_rows, result)
    return forward, result
```

```python
import jax
import jax.numpy as jnp
from jax import lax
from jax.sharding import Mesh, PartitionSpec as P

LEVELS = 4
NX, NZ, NK, NY = 4, 8, 2, 4
HZ = NZ // 2


def cyclic(n, shift):
    return [(i, (i + shift) % n) for i in range(n)]


def swap(v):
    return lax.ppermute(v, "k", [(0, 1), (1, 0)])


def shards(factor, diag_inverse, right_side, levels, pattern):
    n_j, width = factor.shape[1], factor.shape[3]
    n_rhs = right_side.shape[1]
    half = n_rhs // NK
    x, z, k, y = (lax.axis_index(a) for a in ("x", "z", "k", "y"))
    z_even, odd = z % 2, y % 2
    own_row = (x * NZ + z) * NK + k
    l_own = factor.reshape(n_j, width, width)
    d_own = diag_inverse[0]
    b_all = right_side[0].reshape(NK, half, width)
    b_mine = lax.dynamic_index_in_dim(b_all, k, 0, keepdims=False)
    b_theirs = lax.dynamic_index_in_dim(b_all, 1 - k, 0, keepdims=False)
    level_own = lax.dynamic_index_in_dim(levels, own_row, 0, keepdims=False)
    level_par = lax.dynamic_index_in_dim(levels, own_row + 1 - 2 * k, 0, keepdims=False)
    col_levels = lax.dynamic_index_in_dim(levels.reshape(n_j, NY), y, 1, keepdims=False)
    u_own = ((pattern.reshape(n_j) == 1) & (col_levels < level_own)).astype(jnp.bfloat16)

    d_par = swap(d_own)
    b_par = swap(b_theirs)
    u_par = swap(u_own)
    l_par = swap(l_own)

    def solve(v, d):
        return jnp.einsum("kb,ab->ka", v, d, preferred_element_type=jnp.float32).astype(jnp.bfloat16)

    def solve_t(v, d):
        return jnp.einsum("ka,ab->kb", v, d, preferred_element_type=jnp.float32).astype(jnp.bfloat16)

    zero = jnp.zeros((half, width), jnp.bfloat16)
    f_own = jnp.where(level_own == 0, solve(b_mine, d_own), zero)
    f_par = jnp.where(level_par == 0, solve(b_par, d_par), zero)
    p_own = jnp.zeros((half, width), jnp.float32)
    p_par = jnp.zeros((half, width), jnp.float32)
    is_own = k == odd
    level_r = jnp.where(is_own, level_own, level_par)
    for level in range(1, LEVELS):
        f_r = jnp.where(is_own, f_own, f_par)
        sent = jnp.where(level_r == level - 1, f_r, zero)
        got = lax.all_to_all(jnp.broadcast_to(sent[None], (NZ, half, width)), "z", 0, 0)
        got = lax.dynamic_index_in_dim(got.reshape(HZ, 2, half, width), y // 2, 1, keepdims=False)
        parts = [lax.ppermute(got, "x", cyclic(NX, s)) for s in (3, 2, 1)] + [got]
        ring = jnp.concatenate(parts + parts[:-1], 0)
        cols = lax.dynamic_slice_in_dim(ring, (NX - 1 - x) * HZ, n_j, 0)
        p_own = p_own + jnp.einsum("jkb,jab->ka", cols * u_own[:, None, None], l_own, preferred_element_type=jnp.float32)
        p_par = p_par + jnp.einsum("jkb,jab->ka", cols * u_par[:, None, None], l_par, preferred_element_type=jnp.float32)
        rows = jnp.stack([jnp.where(k == 0, p_own, p_par), jnp.where(k == 0, p_par, p_own)]).astype(jnp.bfloat16)
        others = [lax.ppermute(rows, "y", cyclic(NY, s)).astype(jnp.float32) for s in (1, 2, 3)]
        other = others[0] + others[1] + others[2]
        s_own = p_own + jnp.where(k == 0, other[0], other[1])
        s_par = p_par + jnp.where(k == 0, other[1], other[0])
        f_own = jnp.where(level_own == level, solve((b_mine.astype(jnp.float32) - s_own).astype(jnp.bfloat16), d_own), f_own)
        f_par = jnp.where(level_par == level, solve((b_par.astype(jnp.float32) - s_par).astype(jnp.bfloat16), d_par), f_par)

    top = LEVELS - 1
    o_own = jnp.where(level_own == top, solve_t(f_own, d_own), zero)
    o_par = jnp.where(level_par == top, solve_t(f_par, d_par), zero)
    f_r = jnp.where(is_own, f_own, f_par)
    d_r = jnp.where(is_own, d_own, d_par)
    r_sum = jnp.zeros((half, width), jnp.float32)
    for level in range(top - 1, -1, -1):
        m_own = jnp.where(level_own == level + 1, o_own, zero)
        m_par = jnp.where(level_par == level + 1, o_par, zero)
        t = jnp.einsum("jka,jab->jkb", m_own[None] * u_own[:, None, None], l_own, preferred_element_type=jnp.float32)
        t = t + jnp.einsum("jka,jab->jkb", m_par[None] * u_par[:, None, None], l_par, preferred_element_type=jnp.float32)
        t = t.reshape(NX, HZ, half, width)
        mine = lax.dynamic_index_in_dim(t, x, 0, keepdims=False)
        for s in (1, 2, 3):
            piece = lax.dynamic_index_in_dim(t, (x + s) % NX, 0, keepdims=False).astype(jnp.bfloat16)
            mine = mine + lax.ppermute(piece, "x", cyclic(NX, s)).astype(jnp.float32)
        out = jnp.broadcast_to(mine.astype(jnp.bfloat16)[:, None], (HZ, 2, half, width)).reshape(NZ, half, width)
        arrived = lax.all_to_all(out, "z", 0, 0)
        r_sum = r_sum + jnp.sum(arrived.astype(jnp.float32), axis=0)
        o_r = solve_t((f_r.astype(jnp.float32) - r_sum).astype(jnp.bfloat16), d_r)
        got = jnp.stack([o_r] + [lax.ppermute(o_r, "y", cyclic(NY, s)) for s in (1, 2, 3)])
        new_own = lax.dynamic_index_in_dim(got, (y - 2 * z_even - k) % NY, 0, keepdims=False)
        new_par = lax.dynamic_index_in_dim(got, (y - 2 * z_even - 1 + k) % NY, 0, keepdims=False)
        o_own = jnp.where(level_own == level, new_own, o_own)
        o_par = jnp.where(level_par == level, new_par, o_par)

    theirs = swap(jnp.stack([f_par, o_par]))
    mine = jnp.stack([f_own, o_own])
    both = jnp.concatenate([jnp.where(k == 0, mine, theirs), jnp.where(k == 0, theirs, mine)], axis=1)
    return (both[0][None], both[1][None])


def solution(mesh):
    fine = Mesh(mesh.devices.reshape(NX, NZ, NK, NY), ("x", "z", "k", "y"))
    row = ("x", "z", "k")
    return jax.shard_map(
        shards,
        mesh=fine,
        in_specs=(
            P(row, None, "y", None, None),
            P(row, None, None),
            P(row, None, None),
            P(),
            P(row, None, "y"),
        ),
        out_specs=(P(row, None, None), P(row, None, None)),
        check_vma=False,
    )
```

```python
import functools

import jax
import jax.numpy as jnp
from jax import lax
from jax.experimental import pallas as pl
from jax.experimental.pallas import tpu as pltpu
from jax.sharding import Mesh, PartitionSpec as P

LEVELS = 4
NX, NZ, NK, NY = 4, 8, 2, 4
HZ = NZ // 2
F32, BF16 = jnp.float32, jnp.bfloat16
N_PLAN = 2 * NX * HZ
HELD = 20


def cyclic(n, shift):
    return [(i, (i + shift) % n) for i in range(n)]


def swap(v):
    return lax.ppermute(v, "k", [(0, 1), (1, 0)])


def times_transposed(v, d):
    return lax.dot_general(v, d, (((1,), (1,)), ((), ())), preferred_element_type=F32)


def spread_levels(levels, pattern, out, kept):
    x, z, k = (lax.axis_index(a) for a in ("x", "z", "k"))
    for i in range(NX * HZ * NY):
        kept[i] = levels[i]
    for i in range(NX * HZ):
        kept[NX * HZ * NY + i] = pattern[i]
    own = (x * NZ + z) * NK + k
    out[0] = jnp.full(out.shape[1:], levels[own], jnp.int32)
    out[1] = jnp.full(out.shape[1:], levels[own + 1 - 2 * k], jnp.int32)


def make_plan(levels, patterns, plan):
    x, z, k, y = (lax.axis_index(a) for a in ("x", "z", "k", "y"))
    own = (x * NZ + z) * NK + k
    used = jnp.int32(0)
    for r, row in enumerate((own, own + 1 - 2 * k)):
        level = levels[row]
        plan[2 * N_PLAN + r] = level
        for s in range(NX):
            first = lax.rem(x - s + NX, NX) * HZ
            for i in range(HZ):
                n = (r * NX + s) * HZ + i
                col_level = levels[(first + i) * NY + y]
                usable = (patterns[r][first + i] == 1) & (col_level < level)
                plan[n] = jnp.where(usable, 1 + col_level, 0)
                plan[N_PLAN + n] = used
                used = used + jnp.where(usable, 1, 0)
    plan[2 * N_PLAN + 2] = used


def each_block(plan, row_needed, needed, then):
    x = lax.axis_index("x")
    for r in range(2):

        @pl.when(row_needed(plan[2 * N_PLAN + r]))
        def _(r=r):
            for s in range(NX):
                first = lax.rem(x - s + NX, NX) * HZ
                for i in range(HZ):
                    n = (r * NX + s) * HZ + i

                    @pl.when(needed(plan[n]))
                    def _(s=s, i=i, first=first, n=n):
                        then(r, s, i, first + i, plan[N_PLAN + n])


def use_blocks(plan, row_needed, needed, held, l_own, l_par, spare, sem, use):
    def then(r, s, i, j, place):
        @pl.when(place < HELD)
        def _():
            use(r, s, i, held[jnp.minimum(place, HELD - 1)])

        @pl.when(place >= HELD)
        def _():
            copy = pltpu.make_async_copy((l_own, l_par)[r].at[j], spare, sem)
            copy.start()
            copy.wait()
            use(r, s, i, spare[...])

    each_block(plan, row_needed, needed, then)


def add_forward(level, plan, arrived, held, l_own, l_par, spare, sem, p_out, sent):
    def use(r, s, i, block):
        p_out[r] += times_transposed(arrived[s][i], block)

    use_blocks(plan, lambda v: v >= level, lambda v: v == level, held, l_own, l_par, spare, sem, use)
    k = lax.axis_index("k")
    sent[0] = jnp.where(k == 0, p_out[0], p_out[1]).astype(BF16)
    sent[1] = jnp.where(k == 0, p_out[1], p_out[0]).astype(BF16)


def prepare(kept, pattern_par, l_own, l_par, plan, held, sems):
    make_plan(kept, (kept.at[pl.ds(NX * HZ * NY, NX * HZ)], pattern_par), plan)

    def each(then):
        def place_of(r, s, i, j, place):
            @pl.when(place < HELD)
            def _():
                slot = jnp.minimum(place, HELD - 1)
                then(pltpu.make_async_copy((l_own, l_par)[r].at[j], held.at[slot], sems.at[slot]))

        each_block(plan, lambda v: v >= 1, lambda v: v >= 1, place_of)

    each(lambda copy: copy.start())
    each(lambda copy: copy.wait())


def forward_products(level, plan, x0, x1, x2, x3, held, l_own, l_par, p_in, p_out, sent, spare, sem):
    p_out[...] = p_in[...]
    add_forward(level, plan, (x0, x1, x2, x3), held, l_own, l_par, spare, sem, p_out, sent)


def backward_products(level, plan, o_own, o_par, held, l_own, l_par, t0, t1, t2, t3, total, spare, sem):
    solved = (o_own, o_par)
    total[...] = jnp.zeros_like(total)

    def use(r, s, i, block):
        total[s * HZ + i] += jnp.dot(solved[r][...], block, preferred_element_type=F32)

    use_blocks(
        plan, lambda v: v == level + 1, lambda v: (v >= 1) & (v <= level + 1), held, l_own, l_par, spare, sem, use
    )
    t0[...] = total[0:HZ]
    for s, out in ((1, t1), (2, t2), (3, t3)):
        out[...] = total[s * HZ : (s + 1) * HZ].astype(BF16)


def shards(factor, diag_inverse, right_side, levels, pattern):
    n_j, width = factor.shape[1], factor.shape[3]
    n_rhs = right_side.shape[1]
    half = n_rhs // NK
    x, z, k, y = (lax.axis_index(a) for a in ("x", "z", "k", "y"))
    is_own = k == y % 2

    d_own = diag_inverse[0]
    d_par = swap(d_own)
    b_par = swap(right_side[0])
    vmem, smem = pl.BlockSpec(memory_space=pltpu.VMEM), pl.BlockSpec(memory_space=pltpu.SMEM)
    anywhere = pl.BlockSpec(memory_space=pl.ANY)
    params = pltpu.CompilerParams(vmem_limit_bytes=2 << 20)
    pattern = pattern.reshape(n_j)
    row_levels, kept = pl.pallas_call(
        spread_levels,
        in_specs=[smem] * 2,
        out_specs=[vmem, smem],
        out_shape=[jax.ShapeDtypeStruct((2, half, width), jnp.int32), pltpu.SMEM((n_j * (NY + 1),), jnp.int32)],
        compiler_params=params,
    )(levels, pattern)
    kept = pltpu.with_memory_space_constraint(kept, pltpu.SMEM)
    level_own, level_par = row_levels[0], row_levels[1]

    l_own = factor.reshape(n_j, width, width)
    l_own, d_par, b_par = lax.optimization_barrier((l_own, d_par, b_par))
    l_par = swap(l_own)
    l_own, l_par = (pltpu.with_memory_space_constraint(v, pltpu.HBM) for v in (l_own, l_par))

    def my_half(v):
        return lax.dynamic_slice_in_dim(v, k * half, half, 0)

    b_own, b_par = my_half(right_side[0]), my_half(b_par)

    def solve(v, d):
        return jnp.einsum("kb,ab->ka", v.astype(BF16), d, preferred_element_type=F32).astype(BF16)

    def solve_t(v, d):
        return jnp.einsum("ka,ab->kb", v.astype(BF16), d, preferred_element_type=F32).astype(BF16)

    zero = jnp.zeros((half, width), BF16)
    f_own = jnp.where(level_own == 0, solve(b_own, d_own), zero)
    f_par = jnp.where(level_par == 0, solve(b_par, d_par), zero)
    b_own, b_par = b_own.astype(F32), b_par.astype(F32)

    fetch = [pltpu.VMEM((width, width), BF16), pltpu.SemaphoreType.DMA]
    products = [jax.ShapeDtypeStruct((2, half, width), t) for t in (F32, BF16)]
    level_r = jnp.where(is_own, level_own, level_par)
    sums = jnp.zeros((2, half, width), F32)
    pattern_par = swap(pattern)
    for level in range(1, LEVELS):
        f_r = jnp.where(is_own, f_own, f_par)
        sent = jnp.where(level_r == level - 1, f_r, zero)
        got = lax.all_to_all(jnp.broadcast_to(sent[None], (NZ, half, width)), "z", 0, 0)
        if level == 1:
            got, pattern_par = lax.optimization_barrier((got, pattern_par))
        got = lax.dynamic_index_in_dim(got.reshape(HZ, 2, half, width), y // 2, 1, keepdims=False)
        parts = [got] + [lax.ppermute(got, "x", cyclic(NX, s)) for s in (1, 2, 3)]
        if level == 1:
            plan, held = pl.pallas_call(
                prepare,
                in_specs=[smem] * 2 + [anywhere] * 2,
                out_specs=[smem, vmem],
                out_shape=[pltpu.SMEM((2 * N_PLAN + 3,), jnp.int32), pltpu.VMEM((HELD, width, width), BF16)],
                scratch_shapes=[pltpu.SemaphoreType.DMA((HELD,))],
                compiler_params=params,
            )(kept, pattern_par, l_own, l_par)
            plan = pltpu.with_memory_space_constraint(plan, pltpu.SMEM)
            held = pltpu.with_memory_space_constraint(held, pltpu.VMEM)
        sums, rows = pl.pallas_call(
            functools.partial(forward_products, level),
            in_specs=[smem] + [vmem] * 5 + [anywhere] * 2 + [vmem],
            out_specs=[vmem] * 2,
            out_shape=products,
            scratch_shapes=fetch,
            compiler_params=params,
        )(plan, *parts, held, l_own, l_par, sums)
        others = [lax.ppermute(rows, "y", cyclic(NY, s)).astype(F32) for s in (1, 2, 3)]
        other = others[0] + others[1] + others[2]
        s_own = sums[0] + jnp.where(k == 0, other[0], other[1])
        s_par = sums[1] + jnp.where(k == 0, other[1], other[0])
        f_own = jnp.where(level_own == level, solve(b_own - s_own, d_own), f_own)
        f_par = jnp.where(level_par == level, solve(b_par - s_par, d_par), f_par)

    top = LEVELS - 1
    o_own = jnp.where(level_own == top, solve_t(f_own, d_own), zero)
    o_par = jnp.where(level_par == top, solve_t(f_par, d_par), zero)
    f_r = jnp.where(is_own, f_own, f_par)
    d_r = jnp.where(is_own, d_own, d_par)
    o_own, o_par, f_r, d_r = lax.optimization_barrier((o_own, o_par, f_r, d_r))
    r_sum = jnp.zeros((half, width), F32)
    for level in range(top - 1, -1, -1):
        mine, *parts = pl.pallas_call(
            functools.partial(backward_products, level),
            in_specs=[smem] + [vmem] * 3 + [anywhere] * 2,
            out_specs=[vmem] * 4,
            out_shape=[jax.ShapeDtypeStruct((HZ, half, width), t) for t in (F32, BF16, BF16, BF16)],
            scratch_shapes=[pltpu.VMEM((n_j, half, width), F32)] + fetch,
            compiler_params=params,
        )(plan, o_own, o_par, held, l_own, l_par)
        for s in (1, 2, 3):
            mine = mine + lax.ppermute(parts[s - 1], "x", cyclic(NX, NX - s)).astype(F32)
        out = jnp.broadcast_to(mine.astype(BF16)[:, None], (HZ, 2, half, width)).reshape(NZ, half, width)
        arrived = lax.all_to_all(out, "z", 0, 0)
        r_sum = r_sum + jnp.sum(arrived.astype(F32), axis=0)
        o_r = solve_t(f_r.astype(F32) - r_sum, d_r)
        got = jnp.stack([o_r] + [lax.ppermute(o_r, "y", cyclic(NY, s)) for s in (1, 2, 3)])
        new_own = lax.dynamic_index_in_dim(got, (y - 2 * (z % 2) - k) % NY, 0, keepdims=False)
        new_par = lax.dynamic_index_in_dim(got, (y - 2 * (z % 2) - 1 + k) % NY, 0, keepdims=False)
        o_own = jnp.where(level_own == level, new_own, o_own)
        o_par = jnp.where(level_par == level, new_par, o_par)

    theirs = swap(jnp.stack([f_par, o_par]))
    mine = jnp.stack([f_own, o_own])
    both = jnp.concatenate([jnp.where(k == 0, mine, theirs), jnp.where(k == 0, theirs, mine)], axis=1)
    return (both[0][None], both[1][None])


def solution(mesh):
    fine = Mesh(mesh.devices.reshape(NX, NZ, NK, NY), ("x", "z", "k", "y"))
    row = ("x", "z", "k")
    return jax.shard_map(
        shards,
        mesh=fine,
        in_specs=(
            P(row, None, "y", None, None),
            P(row, None, None),
            P(row, None, None),
            P(),
            P(row, None, "y"),
        ),
        out_specs=(P(row, None, None), P(row, None, None)),
        check_vma=False,
    )
```

```python
import functools

import jax
import jax.numpy as jnp
from jax import lax
from jax.experimental import pallas as pl
from jax.experimental.pallas import tpu as pltpu
from jax.sharding import Mesh, PartitionSpec as P

LEVELS = 4
NX, NZ, NK, NY = 4, 8, 2, 4
HZ = NZ // 2
F32, BF16 = jnp.float32, jnp.bfloat16
HELD = 20
BOUNDS = 2 * NX * HZ + 1
ROWS = BOUNDS + 2 * LEVELS + 1


def pairs(n, bits):
    return [(i, i ^ bits) for i in range(n)]


def swap(v):
    return lax.ppermute(v, "k", [(0, 1), (1, 0)])


def times_transposed(v, d):
    return lax.dot_general(v, d, (((1,), (1,)), ((), ())), preferred_element_type=F32)


def fetch_all(moves, sems):
    copies = [pltpu.make_async_copy(source, to, sems.at[i]) for i, (source, to) in enumerate(moves)]
    for copy in copies:
        copy.start()
    for copy in copies:
        copy.wait()


def first_rows(levels_hbm, b_hbm, d_hbm, row_levels, b_own, f_own, levels, d, sems):
    x, z, k = (lax.axis_index(a) for a in ("x", "z", "k"))
    own = (x * NZ + z) * NK + k
    half = b_own.shape[0]
    b_mine = b_hbm.at[pl.ds(pl.multiple_of(k * half, half), half), :]
    fetch_all(((levels_hbm, levels), (b_mine, b_own), (d_hbm, d)), sems)
    level = levels[own]
    row_levels[0] = jnp.full(row_levels.shape[1:], level, jnp.int32)
    row_levels[1] = jnp.full(row_levels.shape[1:], levels[own + 1 - 2 * k], jnp.int32)
    f_own[...] = jnp.where(level == 0, times_transposed(b_own[...], d[...]), 0.0).astype(BF16)


def make_plan(levels, patterns, plan):
    x, z, k, y = (lax.axis_index(a) for a in ("x", "z", "k", "y"))
    own = (x * NZ + z) * NK + k
    used = jnp.int32(0)
    for r, row in enumerate((own, own + 1 - 2 * k)):
        row_level = levels[row]
        plan[ROWS + r] = row_level
        cols = []
        for s in range(NX):
            first = (x ^ s) * HZ
            for i in range(HZ):
                level = levels[(first + i) * NY + y]
                usable = (patterns[r][first + i] == 1) & (level < row_level)
                cols.append(jnp.where(usable, level, LEVELS))
        for level in range(LEVELS):
            plan[BOUNDS + r * LEVELS + level] = used
            if level < LEVELS - 1:
                for n, col in enumerate(cols):
                    plan[used] = r * NX * HZ + n
                    used = used + jnp.where(col == level, 1, 0)
    plan[BOUNDS + 2 * LEVELS] = used


def block_column(x, n):
    return (x ^ (n // HZ)) * HZ + n % HZ


def prepare(levels_hbm, pattern_hbm, pattern_par, l_own, l_par, here, plan, held, rest, passed, levels, pattern_own, sems):
    passed[...] = here[...]
    fetch_all(((levels_hbm, levels), (pattern_hbm, pattern_own)), sems)
    make_plan(levels, (pattern_own, pattern_par), plan)
    x = lax.axis_index("x")

    def each(then):
        def step(place, carry):
            n = plan[place]
            j = block_column(x, n % (NX * HZ))
            for r, blocks in enumerate((l_own, l_par)):
                mine = n // (NX * HZ) == r

                @pl.when(mine & (place < HELD))
                def _():
                    to = held.at[jnp.minimum(place, HELD - 1)]
                    then(pltpu.make_async_copy(blocks.at[j], to, sems.at[place]))

                @pl.when(mine & (place >= HELD))
                def _():
                    to = rest.at[jnp.maximum(place - HELD, 0)]
                    then(pltpu.make_async_copy(blocks.at[j], to, sems.at[place]))

            return carry

        lax.fori_loop(0, plan[BOUNDS + 2 * LEVELS], step, 0)

    each(lambda copy: copy.start())
    each(lambda copy: copy.wait())


def use_blocks(plan, r, first, last, held, rest, spare, sem, use):
    def step(place, carry):
        n = plan[place] - r * NX * HZ

        @pl.when(place < HELD)
        def _():
            use(n, held[jnp.minimum(place, HELD - 1)])

        @pl.when(place >= HELD)
        def _():
            copy = pltpu.make_async_copy(rest.at[jnp.maximum(place - HELD, 0)], spare, sem)
            copy.start()
            copy.wait()
            use(n, spare[...])

        return carry

    lax.fori_loop(first, last, step, 0)


def forward_products(level, plan, arrived, held, rest, p_in, p_out, sent, spare, sem):
    p_out[...] = p_in[...]
    for r in range(2):

        def use(n, block, r=r):
            p_out[r] += times_transposed(arrived[n], block)

        at = BOUNDS + r * LEVELS + level - 1
        use_blocks(plan, r, plan[at], plan[at + 1], held, rest, spare, sem, use)
    k = lax.axis_index("k")
    sent[0] = jnp.where(k == 0, p_out[0], p_out[1]).astype(BF16)
    sent[1] = jnp.where(k == 0, p_out[1], p_out[0]).astype(BF16)


def backward_products(level, plan, o_own, o_par, held, rest, t0, t1, t2, t3, total, spare, sem):
    total[...] = jnp.zeros_like(total)
    for r, solved in enumerate((o_own, o_par)):

        def use(n, block, solved=solved):
            total[n] += jnp.dot(solved[...], block, preferred_element_type=F32)

        @pl.when(plan[ROWS + r] == level + 1)
        def _(r=r, use=use):
            at = BOUNDS + r * LEVELS
            use_blocks(plan, r, plan[at], plan[at + LEVELS], held, rest, spare, sem, use)

    t0[...] = total[0:HZ]
    for s, out in ((1, t1), (2, t2), (3, t3)):
        out[...] = total[s * HZ : (s + 1) * HZ].astype(BF16)


def in_hbm(v):
    return pltpu.with_memory_space_constraint(v, pltpu.HBM)


def shards(factor, diag_inverse, right_side, levels, pattern):
    n_j, width = factor.shape[1], factor.shape[3]
    n_rhs = right_side.shape[1]
    half = n_rhs // NK
    x, z, k, y = (lax.axis_index(a) for a in ("x", "z", "k", "y"))
    is_own = k == y % 2

    d_own = diag_inverse[0]
    d_par = swap(d_own)
    b_par = swap(right_side[0])
    pattern_own = pattern.reshape(n_j)
    pattern_par = swap(pattern_own)
    vmem, smem = pl.BlockSpec(memory_space=pltpu.VMEM), pl.BlockSpec(memory_space=pltpu.SMEM)
    anywhere = pl.BlockSpec(memory_space=pl.ANY)
    params = pltpu.CompilerParams(vmem_limit_bytes=2 << 20)
    row_levels, b_own, f_own = pl.pallas_call(
        first_rows,
        in_specs=[anywhere] * 3,
        out_specs=[vmem] * 3,
        out_shape=[
            jax.ShapeDtypeStruct((2, half, width), jnp.int32),
            jax.ShapeDtypeStruct((half, width), BF16),
            jax.ShapeDtypeStruct((half, width), BF16),
        ],
        scratch_shapes=[
            pltpu.SMEM(levels.shape, jnp.int32),
            pltpu.VMEM((width, width), BF16),
            pltpu.SemaphoreType.DMA((3,)),
        ],
        compiler_params=params,
    )(in_hbm(levels), in_hbm(right_side[0]), in_hbm(d_own))
    l_own = factor.reshape(n_j, width, width)
    l_own, d_par, b_par, pattern_par, row_levels = lax.optimization_barrier((l_own, d_par, b_par, pattern_par, row_levels))
    l_par = in_hbm(swap(l_own))
    l_own = in_hbm(l_own)
    level_own, level_par = row_levels[0], row_levels[1]
    b_par = lax.dynamic_slice_in_dim(b_par, k * half, half, 0)

    def solve(v, d):
        return jnp.einsum("kb,ab->ka", v.astype(BF16), d, preferred_element_type=F32).astype(BF16)

    def solve_t(v, d):
        return jnp.einsum("ka,ab->kb", v.astype(BF16), d, preferred_element_type=F32).astype(BF16)

    zero = jnp.zeros((half, width), BF16)
    f_par = jnp.where(level_par == 0, solve(b_par, d_par), zero)
    b_own, b_par = b_own.astype(F32), b_par.astype(F32)

    fetch = [pltpu.VMEM((width, width), BF16), pltpu.SemaphoreType.DMA]
    products = [jax.ShapeDtypeStruct((2, half, width), t) for t in (F32, BF16)]
    level_r = jnp.where(is_own, level_own, level_par)
    sums = jnp.zeros((2, half, width), F32)
    for level in range(1, LEVELS):
        f_r = jnp.where(is_own, f_own, f_par)
        sent = jnp.where(level_r == level - 1, f_r, zero)
        got = lax.all_to_all(jnp.broadcast_to(sent[None], (NZ, half, width)), "z", 0, 0)
        got = lax.dynamic_index_in_dim(got.reshape(HZ, 2, half, width), y // 2, 1, keepdims=False)
        parts = [got] + [lax.ppermute(got, "x", pairs(NX, s)) for s in (1, 2, 3)]
        if level == 1:
            plan, held, rest, got = pl.pallas_call(
                prepare,
                in_specs=[anywhere] * 2 + [smem] + [anywhere] * 2 + [vmem],
                out_specs=[smem, vmem, anywhere, vmem],
                out_shape=[
                    pltpu.SMEM((ROWS + 2,), jnp.int32),
                    pltpu.VMEM((HELD, width, width), BF16),
                    pltpu.HBM((2 * n_j - HELD, width, width), BF16),
                    jax.ShapeDtypeStruct((HZ, half, width), BF16),
                ],
                scratch_shapes=[
                    pltpu.SMEM(levels.shape, jnp.int32),
                    pltpu.SMEM((n_j,), jnp.int32),
                    pltpu.SemaphoreType.DMA((2 * n_j,)),
                ],
                compiler_params=params,

            )(in_hbm(levels), in_hbm(pattern_own), pattern_par, l_own, l_par, got)
            parts[0] = got
            plan = pltpu.with_memory_space_constraint(plan, pltpu.SMEM)
            held = pltpu.with_memory_space_constraint(held, pltpu.VMEM)
            rest = pltpu.with_memory_space_constraint(rest, pltpu.HBM)
        sums, rows = pl.pallas_call(
            functools.partial(forward_products, level),
            in_specs=[smem] + [vmem] * 2 + [anywhere, vmem],
            out_specs=[vmem] * 2,
            out_shape=products,
            scratch_shapes=fetch,
            compiler_params=params,
        )(plan, jnp.concatenate(parts), held, rest, sums)
        others = [lax.ppermute(rows, "y", pairs(NY, s)).astype(F32) for s in (1, 2, 3)]
        other = others[0] + others[1] + others[2]
        s_own = sums[0] + jnp.where(k == 0, other[0], other[1])
        s_par = sums[1] + jnp.where(k == 0, other[1], other[0])
        f_own = jnp.where(level_own == level, solve(b_own - s_own, d_own), f_own)
        f_par = jnp.where(level_par == level, solve(b_par - s_par, d_par), f_par)

    top = LEVELS - 1
    o_own = jnp.where(level_own == top, solve_t(f_own, d_own), zero)
    o_par = jnp.where(level_par == top, solve_t(f_par, d_par), zero)
    f_r = jnp.where(is_own, f_own, f_par)
    d_r = jnp.where(is_own, d_own, d_par)
    o_own, o_par, f_r, d_r = lax.optimization_barrier((o_own, o_par, f_r, d_r))
    r_sum = jnp.zeros((half, width), F32)
    for level in range(top - 1, -1, -1):
        mine, *parts = pl.pallas_call(
            functools.partial(backward_products, level),
            in_specs=[smem] + [vmem] * 3 + [anywhere],
            out_specs=[vmem] * 4,
            out_shape=[jax.ShapeDtypeStruct((HZ, half, width), t) for t in (F32, BF16, BF16, BF16)],
            scratch_shapes=[pltpu.VMEM((n_j, half, width), F32)] + fetch,
            compiler_params=params,
        )(plan, o_own, o_par, held, rest)
        for s in (1, 2, 3):
            mine = mine + lax.ppermute(parts[s - 1], "x", pairs(NX, s)).astype(F32)
        out = jnp.broadcast_to(mine.astype(BF16)[:, None], (HZ, 2, half, width)).reshape(NZ, half, width)
        arrived = lax.all_to_all(out, "z", 0, 0)
        r_sum = r_sum + jnp.sum(arrived.astype(F32), axis=0)
        o_r = solve_t(f_r.astype(F32) - r_sum, d_r)
        got = jnp.stack([o_r] + [lax.ppermute(o_r, "y", pairs(NY, s)) for s in (1, 2, 3)])
        new_own = lax.dynamic_index_in_dim(got, y ^ (2 * (z % 2) + k), 0, keepdims=False)
        new_par = lax.dynamic_index_in_dim(got, y ^ (2 * (z % 2) + 1 - k), 0, keepdims=False)
        o_own = jnp.where(level_own == level, new_own, o_own)
        o_par = jnp.where(level_par == level, new_par, o_par)

    theirs = swap(jnp.stack([f_par, o_par]))
    mine = jnp.stack([f_own, o_own])
    both = jnp.concatenate([jnp.where(k == 0, mine, theirs), jnp.where(k == 0, theirs, mine)], axis=1)
    return (both[0][None], both[1][None])


def solution(mesh):
    fine = Mesh(mesh.devices.reshape(NX, NZ, NK, NY), ("x", "z", "k", "y"))
    row = ("x", "z", "k")
    return jax.shard_map(
        shards,
        mesh=fine,
        in_specs=(
            P(row, None, "y", None, None),
            P(row, None, None),
            P(row, None, None),
            P(),
            P(row, None, "y"),
        ),
        out_specs=(P(row, None, None), P(row, None, None)),
        check_vma=False,
    )
```

```python
import functools

import jax
import jax.numpy as jnp
from jax import lax
from jax.experimental import pallas as pl
from jax.experimental.pallas import tpu as pltpu
from jax.sharding import Mesh, PartitionSpec as P

LEVELS = 4
NX, NZ, NK, NY = 4, 8, 2, 4
HZ = NZ // 2
F32, BF16 = jnp.float32, jnp.bfloat16
HELD = 20
BOUNDS = 2 * NX * HZ + 1
ROWS = BOUNDS + 2 * LEVELS + 1


def pairs(n, bits):
    return [(i, i ^ bits) for i in range(n)]


def swap(v):
    return lax.ppermute(v, "k", [(0, 1), (1, 0)])


def times_transposed(v, d):
    return lax.dot_general(v, d, (((1,), (1,)), ((), ())), preferred_element_type=F32)


def fetch_all(moves, sems):
    copies = [pltpu.make_async_copy(source, to, sems.at[i]) for i, (source, to) in enumerate(moves)]
    for copy in copies:
        copy.start()
    for copy in copies:
        copy.wait()


def first_rows(levels_hbm, b_hbm, d_hbm, row_levels, b_own, f_own, levels, d, sems):
    x, z, k = (lax.axis_index(a) for a in ("x", "z", "k"))
    own = (x * NZ + z) * NK + k
    half = b_own.shape[0]
    b_mine = b_hbm.at[pl.ds(pl.multiple_of(k * half, half), half), :]
    fetch_all(((levels_hbm, levels), (b_mine, b_own), (d_hbm, d)), sems)
    level = levels[own]
    row_levels[0] = jnp.full(row_levels.shape[1:], level, jnp.int32)
    row_levels[1] = jnp.full(row_levels.shape[1:], levels[own + 1 - 2 * k], jnp.int32)
    f_own[...] = jnp.where(level == 0, times_transposed(b_own[...], d[...]), 0.0).astype(BF16)


def make_plan(levels, patterns, plan):
    x, z, k, y = (lax.axis_index(a) for a in ("x", "z", "k", "y"))
    own = (x * NZ + z) * NK + k
    used = jnp.int32(0)
    for r, row in enumerate((own, own + 1 - 2 * k)):
        row_level = levels[row]
        plan[ROWS + r] = row_level
        cols = []
        for s in range(NX):
            first = (x ^ s) * HZ
            for i in range(HZ):
                level = levels[(first + i) * NY + y]
                usable = (patterns[r][first + i] == 1) & (level < row_level)
                cols.append(jnp.where(usable, level, LEVELS))
        for level in range(LEVELS):
            plan[BOUNDS + r * LEVELS + level] = used
            if level < LEVELS - 1:
                for n, col in enumerate(cols):
                    plan[used] = r * NX * HZ + n
                    used = used + jnp.where(col == level, 1, 0)
    plan[BOUNDS + 2 * LEVELS] = used


def block_column(x, n):
    return (x ^ (n // HZ)) * HZ + n % HZ


def prepare(levels_hbm, pattern_hbm, pattern_par, l_own, l_par, here, plan, held, rest, passed, levels, pattern_own, sems):
    passed[...] = here[...]
    fetch_all(((levels_hbm, levels), (pattern_hbm, pattern_own)), sems)
    make_plan(levels, (pattern_own, pattern_par), plan)
    x = lax.axis_index("x")

    def each(then):
        def step(place, carry):
            n = plan[place]
            j = block_column(x, n % (NX * HZ))
            for r, blocks in enumerate((l_own, l_par)):
                mine = n // (NX * HZ) == r

                @pl.when(mine & (place < HELD))
                def _():
                    to = held.at[jnp.minimum(place, HELD - 1)]
                    then(pltpu.make_async_copy(blocks.at[j], to, sems.at[place]))

                @pl.when(mine & (place >= HELD))
                def _():
                    to = rest.at[jnp.maximum(place - HELD, 0)]
                    then(pltpu.make_async_copy(blocks.at[j], to, sems.at[place]))

            return carry

        lax.fori_loop(0, plan[BOUNDS + 2 * LEVELS], step, 0)

    each(lambda copy: copy.start())
    each(lambda copy: copy.wait())


def use_blocks(plan, r, first, last, held, rest, spare, sem, use):
    def step(place, carry):
        n = plan[place] - r * NX * HZ

        @pl.when(place < HELD)
        def _():
            use(n, held[jnp.minimum(place, HELD - 1)])

        @pl.when(place >= HELD)
        def _():
            copy = pltpu.make_async_copy(rest.at[jnp.maximum(place - HELD, 0)], spare, sem)
            copy.start()
            copy.wait()
            use(n, spare[...])

        return carry

    lax.fori_loop(first, last, step, 0)


def forward_products(level, plan, arrived, held, rest, p_in, p_out, sent, spare, sem):
    p_out[...] = p_in[...]
    for r in range(2):

        def use(n, block, r=r):
            p_out[r] += times_transposed(arrived[n], block)

        at = BOUNDS + r * LEVELS + level - 1
        use_blocks(plan, r, plan[at], plan[at + 1], held, rest, spare, sem, use)
    k = lax.axis_index("k")
    sent[0] = jnp.where(k == 0, p_out[0], p_out[1]).astype(BF16)
    sent[1] = jnp.where(k == 0, p_out[1], p_out[0]).astype(BF16)


def backward_products(level, plan, o_own, o_par, held, rest, sent, total, spare, sem):
    x = lax.axis_index("x")
    total[...] = jnp.zeros_like(total)
    for r, solved in enumerate((o_own, o_par)):

        def use(n, block, solved=solved):
            total[block_column(x, n)] += jnp.dot(solved[...], block, preferred_element_type=F32)

        @pl.when(plan[ROWS + r] == level + 1)
        def _(r=r, use=use):
            at = BOUNDS + r * LEVELS
            use_blocks(plan, r, plan[at], plan[at + LEVELS], held, rest, spare, sem, use)

    for j in range(NX * HZ):
        rows = total[j].astype(BF16)
        sent[2 * j] = rows
        sent[2 * j + 1] = rows


def in_hbm(v):
    return pltpu.with_memory_space_constraint(v, pltpu.HBM)


def shards(factor, diag_inverse, right_side, levels, pattern):
    n_j, width = factor.shape[1], factor.shape[3]
    n_rhs = right_side.shape[1]
    half = n_rhs // NK
    x, z, k, y = (lax.axis_index(a) for a in ("x", "z", "k", "y"))
    is_own = k == y % 2

    d_own = diag_inverse[0]
    d_par = swap(d_own)
    b_par = swap(right_side[0])
    pattern_own = pattern.reshape(n_j)
    pattern_par = swap(pattern_own)
    vmem, smem = pl.BlockSpec(memory_space=pltpu.VMEM), pl.BlockSpec(memory_space=pltpu.SMEM)
    anywhere = pl.BlockSpec(memory_space=pl.ANY)
    params = pltpu.CompilerParams(vmem_limit_bytes=2 << 20)
    row_levels, b_own, f_own = pl.pallas_call(
        first_rows,
        in_specs=[anywhere] * 3,
        out_specs=[vmem] * 3,
        out_shape=[
            jax.ShapeDtypeStruct((2, half, width), jnp.int32),
            jax.ShapeDtypeStruct((half, width), BF16),
            jax.ShapeDtypeStruct((half, width), BF16),
        ],
        scratch_shapes=[
            pltpu.SMEM(levels.shape, jnp.int32),
            pltpu.VMEM((width, width), BF16),
            pltpu.SemaphoreType.DMA((3,)),
        ],
        compiler_params=params,
    )(in_hbm(levels), in_hbm(right_side[0]), in_hbm(d_own))
    l_own = factor.reshape(n_j, width, width)
    l_own, d_par, b_par, pattern_par, row_levels = lax.optimization_barrier((l_own, d_par, b_par, pattern_par, row_levels))
    l_par = in_hbm(swap(l_own))
    l_own = in_hbm(l_own)
    level_own, level_par = row_levels[0], row_levels[1]
    b_par = lax.dynamic_slice_in_dim(b_par, k * half, half, 0)

    def solve(v, d):
        return jnp.einsum("kb,ab->ka", v.astype(BF16), d, preferred_element_type=F32).astype(BF16)

    def solve_t(v, d):
        return jnp.einsum("ka,ab->kb", v.astype(BF16), d, preferred_element_type=F32).astype(BF16)

    zero = jnp.zeros((half, width), BF16)
    f_par = jnp.where(level_par == 0, solve(b_par, d_par), zero)
    b_own, b_par = b_own.astype(F32), b_par.astype(F32)

    fetch = [pltpu.VMEM((width, width), BF16), pltpu.SemaphoreType.DMA]
    products = [jax.ShapeDtypeStruct((2, half, width), t) for t in (F32, BF16)]
    level_r = jnp.where(is_own, level_own, level_par)
    sums = jnp.zeros((2, half, width), F32)
    for level in range(1, LEVELS):
        f_r = jnp.where(is_own, f_own, f_par)
        sent = jnp.where(level_r == level - 1, f_r, zero)
        got = lax.all_to_all(jnp.broadcast_to(sent[None], (NZ, half, width)), "z", 0, 0)
        got = lax.dynamic_index_in_dim(got.reshape(HZ, 2, half, width), y // 2, 1, keepdims=False)
        parts = [got] + [lax.ppermute(got, "x", pairs(NX, s)) for s in (1, 2, 3)]
        if level == 1:
            plan, held, rest, got = pl.pallas_call(
                prepare,
                in_specs=[anywhere] * 2 + [smem] + [anywhere] * 2 + [vmem],
                out_specs=[smem, vmem, anywhere, vmem],
                out_shape=[
                    pltpu.SMEM((ROWS + 2,), jnp.int32),
                    pltpu.VMEM((HELD, width, width), BF16),
                    pltpu.HBM((2 * n_j - HELD, width, width), BF16),
                    jax.ShapeDtypeStruct((HZ, half, width), BF16),
                ],
                scratch_shapes=[
                    pltpu.SMEM(levels.shape, jnp.int32),
                    pltpu.SMEM((n_j,), jnp.int32),
                    pltpu.SemaphoreType.DMA((2 * n_j,)),
                ],
                compiler_params=params,

            )(in_hbm(levels), in_hbm(pattern_own), pattern_par, l_own, l_par, got)
            parts[0] = got
            plan = pltpu.with_memory_space_constraint(plan, pltpu.SMEM)
            held = pltpu.with_memory_space_constraint(held, pltpu.VMEM)
            rest = pltpu.with_memory_space_constraint(rest, pltpu.HBM)
        sums, rows = pl.pallas_call(
            functools.partial(forward_products, level),
            in_specs=[smem] + [vmem] * 2 + [anywhere, vmem],
            out_specs=[vmem] * 2,
            out_shape=products,
            scratch_shapes=fetch,
            compiler_params=params,
        )(plan, jnp.concatenate(parts), held, rest, sums)
        others = [lax.ppermute(rows, "y", pairs(NY, s)).astype(F32) for s in (1, 2, 3)]
        other = others[0] + others[1] + others[2]
        s_own = sums[0] + jnp.where(k == 0, other[0], other[1])
        s_par = sums[1] + jnp.where(k == 0, other[1], other[0])
        f_own = jnp.where(level_own == level, solve(b_own - s_own, d_own), f_own)
        f_par = jnp.where(level_par == level, solve(b_par - s_par, d_par), f_par)

    top = LEVELS - 1
    o_own = jnp.where(level_own == top, solve_t(f_own, d_own), zero)
    o_par = jnp.where(level_par == top, solve_t(f_par, d_par), zero)
    f_r = jnp.where(is_own, f_own, f_par)
    d_r = jnp.where(is_own, d_own, d_par)
    o_own, o_par, f_r, d_r = lax.optimization_barrier((o_own, o_par, f_r, d_r))
    r_sum = jnp.zeros((half, width), F32)
    for level in range(top - 1, -1, -1):
        sent = pl.pallas_call(
            functools.partial(backward_products, level),
            in_specs=[smem] + [vmem] * 3 + [anywhere],
            out_specs=vmem,
            out_shape=jax.ShapeDtypeStruct((NX * NZ, half, width), BF16),
            scratch_shapes=[pltpu.VMEM((n_j, half, width), F32)] + fetch,
            compiler_params=params,
        )(plan, o_own, o_par, held, rest)
        arrived = lax.all_to_all(sent, ("x", "z"), 0, 0)
        r_sum = r_sum + jnp.sum(arrived.astype(F32), axis=0)
        o_r = solve_t(f_r.astype(F32) - r_sum, d_r)
        got = jnp.stack([o_r] + [lax.ppermute(o_r, "y", pairs(NY, s)) for s in (1, 2, 3)])
        new_own = lax.dynamic_index_in_dim(got, y ^ (2 * (z % 2) + k), 0, keepdims=False)
        new_par = lax.dynamic_index_in_dim(got, y ^ (2 * (z % 2) + 1 - k), 0, keepdims=False)
        o_own = jnp.where(level_own == level, new_own, o_own)
        o_par = jnp.where(level_par == level, new_par, o_par)

    theirs = swap(jnp.stack([f_par, o_par]))
    mine = jnp.stack([f_own, o_own])
    both = jnp.concatenate([jnp.where(k == 0, mine, theirs), jnp.where(k == 0, theirs, mine)], axis=1)
    return (both[0][None], both[1][None])


def solution(mesh):
    fine = Mesh(mesh.devices.reshape(NX, NZ, NK, NY), ("x", "z", "k", "y"))
    row = ("x", "z", "k")
    return jax.shard_map(
        shards,
        mesh=fine,
        in_specs=(
            P(row, None, "y", None, None),
            P(row, None, None),
            P(row, None, None),
            P(),
            P(row, None, "y"),
        ),
        out_specs=(P(row, None, None), P(row, None, None)),
        check_vma=False,
    )
```

```python
import functools

import jax
import jax.numpy as jnp
from jax import lax
from jax.experimental import pallas as pl
from jax.experimental.pallas import tpu as pltpu
from jax.sharding import Mesh, PartitionSpec as P

LEVELS = 4
NX, NZ, NK, NY = 4, 8, 2, 4
HZ = NZ // 2
F32, BF16 = jnp.float32, jnp.bfloat16
HELD = 20
BOUNDS = 2 * NX * HZ + 1
ROWS = BOUNDS + 2 * LEVELS + 1


def pairs(n, bits):
    return [(i, i ^ bits) for i in range(n)]


def swap(v):
    return lax.ppermute(v, "k", [(0, 1), (1, 0)])


def times_transposed(v, d):
    return lax.dot_general(v, d, (((1,), (1,)), ((), ())), preferred_element_type=F32)


def fetch_all(moves, sems):
    copies = [pltpu.make_async_copy(source, to, sems.at[i]) for i, (source, to) in enumerate(moves)]
    for copy in copies:
        copy.start()
    for copy in copies:
        copy.wait()


def first_rows(levels_hbm, b_hbm, d_hbm, row_levels, b_own, f_own, levels, d, sems):
    x, z, k = (lax.axis_index(a) for a in ("x", "z", "k"))
    own = (x * NZ + z) * NK + k
    half = b_own.shape[0]
    b_mine = b_hbm.at[pl.ds(pl.multiple_of(k * half, half), half), :]
    fetch_all(((levels_hbm, levels), (b_mine, b_own), (d_hbm, d)), sems)
    level = levels[own]
    row_levels[0] = jnp.full(row_levels.shape[1:], level, jnp.int32)
    row_levels[1] = jnp.full(row_levels.shape[1:], levels[own + 1 - 2 * k], jnp.int32)
    f_own[...] = jnp.where(level == 0, times_transposed(b_own[...], d[...]), 0.0).astype(BF16)


def make_plan(levels, patterns, plan):
    x, z, k, y = (lax.axis_index(a) for a in ("x", "z", "k", "y"))
    own = (x * NZ + z) * NK + k
    used = jnp.int32(0)
    for r, row in enumerate((own, own + 1 - 2 * k)):
        row_level = levels[row]
        plan[ROWS + r] = row_level
        cols = []
        for s in range(NX):
            first = (x ^ s) * HZ
            for i in range(HZ):
                level = levels[(first + i) * NY + y]
                usable = (patterns[r][first + i] == 1) & (level < row_level)
                cols.append(jnp.where(usable, level, LEVELS))
        for level in range(LEVELS):
            plan[BOUNDS + r * LEVELS + level] = used
            if level < LEVELS - 1:
                for n, col in enumerate(cols):
                    plan[used] = r * NX * HZ + n
                    used = used + jnp.where(col == level, 1, 0)
    plan[BOUNDS + 2 * LEVELS] = used


def block_column(x, n):
    return (x ^ (n // HZ)) * HZ + n % HZ


def prepare(levels_hbm, pattern_hbm, pattern_par, l_own, l_par, here, plan, held, rest, passed, levels, pattern_own, sems):
    passed[...] = here[...]
    fetch_all(((levels_hbm, levels), (pattern_hbm, pattern_own)), sems)
    make_plan(levels, (pattern_own, pattern_par), plan)
    x = lax.axis_index("x")

    def each(then):
        def step(place, carry):
            n = plan[place]
            j = block_column(x, n % (NX * HZ))
            for r, blocks in enumerate((l_own, l_par)):
                mine = n // (NX * HZ) == r

                @pl.when(mine & (place < HELD))
                def _():
                    to = held.at[jnp.minimum(place, HELD - 1)]
                    then(pltpu.make_async_copy(blocks.at[j], to, sems.at[place]))

                @pl.when(mine & (place >= HELD))
                def _():
                    to = rest.at[jnp.maximum(place - HELD, 0)]
                    then(pltpu.make_async_copy(blocks.at[j], to, sems.at[place]))

            return carry

        lax.fori_loop(0, plan[BOUNDS + 2 * LEVELS], step, 0)

    each(lambda copy: copy.start())
    each(lambda copy: copy.wait())


def use_blocks(plan, r, first, last, held, rest, spare, sem, use):
    def step(place, carry):
        n = plan[place] - r * NX * HZ

        @pl.when(place < HELD)
        def _():
            use(n, held[jnp.minimum(place, HELD - 1)])

        @pl.when(place >= HELD)
        def _():
            copy = pltpu.make_async_copy(rest.at[jnp.maximum(place - HELD, 0)], spare, sem)
            copy.start()
            copy.wait()
            use(n, spare[...])

        return carry

    lax.fori_loop(first, last, step, 0)


def forward_products(level, plan, arrived, held, rest, p_in, p_out, sent, spare, sem):
    x = lax.axis_index("x")
    p_out[...] = p_in[...]
    for r in range(2):

        def use(n, block, r=r):
            p_out[r] += times_transposed(arrived[n if level == 1 else block_column(x, n)], block)

        at = BOUNDS + r * LEVELS + level - 1
        use_blocks(plan, r, plan[at], plan[at + 1], held, rest, spare, sem, use)
    k = lax.axis_index("k")
    sent[0] = jnp.where(k == 0, p_out[0], p_out[1]).astype(BF16)
    sent[1] = jnp.where(k == 0, p_out[1], p_out[0]).astype(BF16)


def backward_products(level, plan, o_own, o_par, held, rest, sent, total, spare, sem):
    x = lax.axis_index("x")
    total[...] = jnp.zeros_like(total)
    for r, solved in enumerate((o_own, o_par)):

        def use(n, block, solved=solved):
            total[block_column(x, n)] += jnp.dot(solved[...], block, preferred_element_type=F32)

        @pl.when(plan[ROWS + r] == level + 1)
        def _(r=r, use=use):
            at = BOUNDS + r * LEVELS
            use_blocks(plan, r, plan[at], plan[at + LEVELS], held, rest, spare, sem, use)

    for j in range(NX * HZ):
        rows = total[j].astype(BF16)
        sent[2 * j] = rows
        sent[2 * j + 1] = rows


def in_hbm(v):
    return pltpu.with_memory_space_constraint(v, pltpu.HBM)


def shards(factor, diag_inverse, right_side, levels, pattern):
    n_j, width = factor.shape[1], factor.shape[3]
    n_rhs = right_side.shape[1]
    half = n_rhs // NK
    x, z, k, y = (lax.axis_index(a) for a in ("x", "z", "k", "y"))
    is_own = k == y % 2

    d_own = diag_inverse[0]
    d_par = swap(d_own)
    b_par = swap(right_side[0])
    pattern_own = pattern.reshape(n_j)
    pattern_par = swap(pattern_own)
    vmem, smem = pl.BlockSpec(memory_space=pltpu.VMEM), pl.BlockSpec(memory_space=pltpu.SMEM)
    anywhere = pl.BlockSpec(memory_space=pl.ANY)
    params = pltpu.CompilerParams(vmem_limit_bytes=2 << 20)
    row_levels, b_own, f_own = pl.pallas_call(
        first_rows,
        in_specs=[anywhere] * 3,
        out_specs=[vmem] * 3,
        out_shape=[
            jax.ShapeDtypeStruct((2, half, width), jnp.int32),
            jax.ShapeDtypeStruct((half, width), BF16),
            jax.ShapeDtypeStruct((half, width), BF16),
        ],
        scratch_shapes=[
            pltpu.SMEM(levels.shape, jnp.int32),
            pltpu.VMEM((width, width), BF16),
            pltpu.SemaphoreType.DMA((3,)),
        ],
        compiler_params=params,
    )(in_hbm(levels), in_hbm(right_side[0]), in_hbm(d_own))
    l_own = factor.reshape(n_j, width, width)
    l_own, d_par, b_par, pattern_par, row_levels = lax.optimization_barrier((l_own, d_par, b_par, pattern_par, row_levels))
    l_par = in_hbm(swap(l_own))
    l_own = in_hbm(l_own)
    level_own, level_par = row_levels[0], row_levels[1]
    b_par = lax.dynamic_slice_in_dim(b_par, k * half, half, 0)

    def solve(v, d):
        return jnp.einsum("kb,ab->ka", v.astype(BF16), d, preferred_element_type=F32).astype(BF16)

    def solve_t(v, d):
        return jnp.einsum("ka,ab->kb", v.astype(BF16), d, preferred_element_type=F32).astype(BF16)

    zero = jnp.zeros((half, width), BF16)
    f_par = jnp.where(level_par == 0, solve(b_par, d_par), zero)
    b_own, b_par = b_own.astype(F32), b_par.astype(F32)

    fetch = [pltpu.VMEM((width, width), BF16), pltpu.SemaphoreType.DMA]
    products = [jax.ShapeDtypeStruct((2, half, width), t) for t in (F32, BF16)]
    level_r = jnp.where(is_own, level_own, level_par)
    sums = jnp.zeros((2, half, width), F32)
    for level in range(1, LEVELS):
        f_r = jnp.where(is_own, f_own, f_par)
        sent = jnp.where(level_r == level - 1, f_r, zero)
        if level == 1:
            got = lax.all_to_all(jnp.broadcast_to(sent[None], (NZ, half, width)), "z", 0, 0)
            got = lax.dynamic_index_in_dim(got.reshape(HZ, 2, half, width), y // 2, 1, keepdims=False)
            parts = [got] + [lax.ppermute(got, "x", pairs(NX, s)) for s in (1, 2, 3)]
        else:
            got = lax.all_to_all(jnp.broadcast_to(sent[None], (NX * NZ, half, width)), ("x", "z"), 0, 0)
            parts = [lax.dynamic_index_in_dim(got.reshape(n_j, 2, half, width), y // 2, 1, keepdims=False)]
        if level == 1:
            plan, held, rest, got = pl.pallas_call(
                prepare,
                in_specs=[anywhere] * 2 + [smem] + [anywhere] * 2 + [vmem],
                out_specs=[smem, vmem, anywhere, vmem],
                out_shape=[
                    pltpu.SMEM((ROWS + 2,), jnp.int32),
                    pltpu.VMEM((HELD, width, width), BF16),
                    pltpu.HBM((2 * n_j - HELD, width, width), BF16),
                    jax.ShapeDtypeStruct((HZ, half, width), BF16),
                ],
                scratch_shapes=[
                    pltpu.SMEM(levels.shape, jnp.int32),
                    pltpu.SMEM((n_j,), jnp.int32),
                    pltpu.SemaphoreType.DMA((2 * n_j,)),
                ],
                compiler_params=params,

            )(in_hbm(levels), in_hbm(pattern_own), pattern_par, l_own, l_par, got)
            parts[0] = got
            plan = pltpu.with_memory_space_constraint(plan, pltpu.SMEM)
            held = pltpu.with_memory_space_constraint(held, pltpu.VMEM)
            rest = pltpu.with_memory_space_constraint(rest, pltpu.HBM)
        sums, rows = pl.pallas_call(
            functools.partial(forward_products, level),
            in_specs=[smem] + [vmem] * 2 + [anywhere, vmem],
            out_specs=[vmem] * 2,
            out_shape=products,
            scratch_shapes=fetch,
            compiler_params=params,
        )(plan, jnp.concatenate(parts), held, rest, sums)
        others = [lax.ppermute(rows, "y", pairs(NY, s)).astype(F32) for s in (1, 2, 3)]
        other = others[0] + others[1] + others[2]
        s_own = sums[0] + jnp.where(k == 0, other[0], other[1])
        s_par = sums[1] + jnp.where(k == 0, other[1], other[0])
        f_own = jnp.where(level_own == level, solve(b_own - s_own, d_own), f_own)
        f_par = jnp.where(level_par == level, solve(b_par - s_par, d_par), f_par)

    top = LEVELS - 1
    o_own = jnp.where(level_own == top, solve_t(f_own, d_own), zero)
    o_par = jnp.where(level_par == top, solve_t(f_par, d_par), zero)
    f_r = jnp.where(is_own, f_own, f_par)
    d_r = jnp.where(is_own, d_own, d_par)
    o_own, o_par, f_r, d_r = lax.optimization_barrier((o_own, o_par, f_r, d_r))
    r_sum = jnp.zeros((half, width), F32)
    for level in range(top - 1, -1, -1):
        sent = pl.pallas_call(
            functools.partial(backward_products, level),
            in_specs=[smem] + [vmem] * 3 + [anywhere],
            out_specs=vmem,
            out_shape=jax.ShapeDtypeStruct((NX * NZ, half, width), BF16),
            scratch_shapes=[pltpu.VMEM((n_j, half, width), F32)] + fetch,
            compiler_params=params,
        )(plan, o_own, o_par, held, rest)
        arrived = lax.all_to_all(sent, ("x", "z"), 0, 0)
        r_sum = r_sum + jnp.sum(arrived.astype(F32), axis=0)
        o_r = solve_t(f_r.astype(F32) - r_sum, d_r)
        got = jnp.stack([o_r] + [lax.ppermute(o_r, "y", pairs(NY, s)) for s in (1, 2, 3)])
        new_own = lax.dynamic_index_in_dim(got, y ^ (2 * (z % 2) + k), 0, keepdims=False)
        new_par = lax.dynamic_index_in_dim(got, y ^ (2 * (z % 2) + 1 - k), 0, keepdims=False)
        o_own = jnp.where(level_own == level, new_own, o_own)
        o_par = jnp.where(level_par == level, new_par, o_par)

    theirs = swap(jnp.stack([f_par, o_par]))
    mine = jnp.stack([f_own, o_own])
    both = jnp.concatenate([jnp.where(k == 0, mine, theirs), jnp.where(k == 0, theirs, mine)], axis=1)
    return (both[0][None], both[1][None])


def solution(mesh):
    fine = Mesh(mesh.devices.reshape(NX, NZ, NK, NY), ("x", "z", "k", "y"))
    row = ("x", "z", "k")
    return jax.shard_map(
        shards,
        mesh=fine,
        in_specs=(
            P(row, None, "y", None, None),
            P(row, None, None),
            P(row, None, None),
            P(),
            P(row, None, "y"),
        ),
        out_specs=(P(row, None, None), P(row, None, None)),
        check_vma=False,
    )
```

```python
import functools

import jax
import jax.numpy as jnp
from jax import lax
from jax.experimental import pallas as pl
from jax.experimental.pallas import tpu as pltpu
from jax.sharding import Mesh, PartitionSpec as P

LEVELS = 4
NX, NZ, NK, NY = 4, 8, 2, 4
HZ = NZ // 2
F32, BF16 = jnp.float32, jnp.bfloat16
HELD = 20
BOUNDS = 2 * NX * HZ + 1
ROWS = BOUNDS + 2 * LEVELS + 1


def pairs(n, bits):
    return [(i, i ^ bits) for i in range(n)]


def swap(v):
    return lax.ppermute(v, "k", [(0, 1), (1, 0)])


def times_transposed(v, d):
    return lax.dot_general(v, d, (((1,), (1,)), ((), ())), preferred_element_type=F32)


def fetch_all(moves, sems):
    copies = [pltpu.make_async_copy(source, to, sems.at[i]) for i, (source, to) in enumerate(moves)]
    for copy in copies:
        copy.start()
    for copy in copies:
        copy.wait()


def first_rows(levels_hbm, b_hbm, d_hbm, row_levels, b_own, f_own, levels, d, sems):
    x, z, k = (lax.axis_index(a) for a in ("x", "z", "k"))
    own = (x * NZ + z) * NK + k
    half = b_own.shape[0]
    b_mine = b_hbm.at[pl.ds(pl.multiple_of(k * half, half), half), :]
    fetch_all(((levels_hbm, levels), (b_mine, b_own), (d_hbm, d)), sems)
    level = levels[own]
    row_levels[0] = jnp.full(row_levels.shape[1:], level, jnp.int32)
    row_levels[1] = jnp.full(row_levels.shape[1:], levels[own + 1 - 2 * k], jnp.int32)
    f_own[...] = jnp.where(level == 0, times_transposed(b_own[...], d[...]), 0.0).astype(BF16)


def make_plan(levels, patterns, plan):
    x, z, k, y = (lax.axis_index(a) for a in ("x", "z", "k", "y"))
    own = (x * NZ + z) * NK + k
    used = jnp.int32(0)
    for r, row in enumerate((own, own + 1 - 2 * k)):
        row_level = levels[row]
        plan[ROWS + r] = row_level
        cols = []
        for s in range(NX):
            first = (x ^ s) * HZ
            for i in range(HZ):
                level = levels[(first + i) * NY + y]
                usable = (patterns[r][first + i] == 1) & (level < row_level)
                cols.append(jnp.where(usable, level, LEVELS))
        for level in range(LEVELS):
            plan[BOUNDS + r * LEVELS + level] = used
            if level < LEVELS - 1:
                for n, col in enumerate(cols):
                    plan[used] = r * NX * HZ + n
                    used = used + jnp.where(col == level, 1, 0)
    plan[BOUNDS + 2 * LEVELS] = used


def block_column(x, n):
    return (x ^ (n // HZ)) * HZ + n % HZ


def prepare(levels_hbm, pattern_hbm, pattern_par, l_own, l_par, here, plan, held, rest, passed, levels, pattern_own, sems):
    passed[...] = here[...]
    fetch_all(((levels_hbm, levels), (pattern_hbm, pattern_own)), sems)
    make_plan(levels, (pattern_own, pattern_par), plan)
    x = lax.axis_index("x")

    def each(then):
        def step(place, carry):
            n = plan[place]
            j = block_column(x, n % (NX * HZ))
            for r, blocks in enumerate((l_own, l_par)):
                mine = n // (NX * HZ) == r

                @pl.when(mine & (place < HELD))
                def _():
                    to = held.at[jnp.minimum(place, HELD - 1)]
                    then(pltpu.make_async_copy(blocks.at[j], to, sems.at[place]))

                @pl.when(mine & (place >= HELD))
                def _():
                    to = rest.at[jnp.maximum(place - HELD, 0)]
                    then(pltpu.make_async_copy(blocks.at[j], to, sems.at[place]))

            return carry

        lax.fori_loop(0, plan[BOUNDS + 2 * LEVELS], step, 0)

    each(lambda copy: copy.start())
    each(lambda copy: copy.wait())


def use_blocks(plan, r, first, last, held, rest, spare, sem, use):
    def step(place, carry):
        n = plan[place] - r * NX * HZ

        @pl.when(place < HELD)
        def _():
            use(n, held[jnp.minimum(place, HELD - 1)])

        @pl.when(place >= HELD)
        def _():
            copy = pltpu.make_async_copy(rest.at[jnp.maximum(place - HELD, 0)], spare, sem)
            copy.start()
            copy.wait()
            use(n, spare[...])

        return carry

    lax.fori_loop(first, last, step, 0)


def forward_products(level, plan, arrived, held, rest, p_in, p_out, sent, spare, sem):
    x = lax.axis_index("x")
    p_out[...] = p_in[...]
    for r in range(2):

        def use(n, block, r=r):
            p_out[r] += times_transposed(arrived[n if level == 1 else block_column(x, n)], block)

        at = BOUNDS + r * LEVELS + level - 1
        use_blocks(plan, r, plan[at], plan[at + 1], held, rest, spare, sem, use)
    k = lax.axis_index("k")
    sent[0] = jnp.where(k == 0, p_out[0], p_out[1]).astype(BF16)
    sent[1] = jnp.where(k == 0, p_out[1], p_out[0]).astype(BF16)


def backward_products(level, plan, o_own, o_par, held, rest, sent, total, spare, sem):
    x = lax.axis_index("x")
    total[...] = jnp.zeros_like(total)
    for r, solved in enumerate((o_own, o_par)):

        def use(n, block, solved=solved):
            total[block_column(x, n)] += jnp.dot(solved[...], block, preferred_element_type=F32)

        @pl.when(plan[ROWS + r] == level + 1)
        def _(r=r, use=use):
            at = BOUNDS + r * LEVELS
            use_blocks(plan, r, plan[at], plan[at + LEVELS], held, rest, spare, sem, use)

    for j in range(NX * HZ):
        rows = total[j].astype(BF16)
        sent[2 * j] = rows
        sent[2 * j + 1] = rows


def in_hbm(v):
    return pltpu.with_memory_space_constraint(v, pltpu.HBM)


def shards(factor, diag_inverse, right_side, levels, pattern):
    n_j, width = factor.shape[1], factor.shape[3]
    n_rhs = right_side.shape[1]
    half = n_rhs // NK
    x, z, k, y = (lax.axis_index(a) for a in ("x", "z", "k", "y"))
    is_own = k == y % 2

    d_own = diag_inverse[0]
    d_par = swap(d_own)
    b_par = swap(right_side[0])
    pattern_own = pattern.reshape(n_j)
    pattern_par = swap(pattern_own)
    vmem, smem = pl.BlockSpec(memory_space=pltpu.VMEM), pl.BlockSpec(memory_space=pltpu.SMEM)
    anywhere = pl.BlockSpec(memory_space=pl.ANY)
    params = pltpu.CompilerParams(vmem_limit_bytes=2 << 20)
    row_levels, b_own, f_own = pl.pallas_call(
        first_rows,
        in_specs=[anywhere] * 3,
        out_specs=[vmem] * 3,
        out_shape=[
            jax.ShapeDtypeStruct((2, half, width), jnp.int32),
            jax.ShapeDtypeStruct((half, width), BF16),
            jax.ShapeDtypeStruct((half, width), BF16),
        ],
        scratch_shapes=[
            pltpu.SMEM(levels.shape, jnp.int32),
            pltpu.VMEM((width, width), BF16),
            pltpu.SemaphoreType.DMA((3,)),
        ],
        compiler_params=params,
    )(in_hbm(levels), in_hbm(right_side[0]), in_hbm(d_own))
    l_own = factor.reshape(n_j, width, width)
    l_own, d_par, b_par, pattern_par, row_levels = lax.optimization_barrier((l_own, d_par, b_par, pattern_par, row_levels))
    l_par = in_hbm(swap(l_own))
    l_own = in_hbm(l_own)
    level_own, level_par = row_levels[0], row_levels[1]
    b_par = lax.dynamic_slice_in_dim(b_par, k * half, half, 0)

    def solve(v, d):
        return jnp.einsum("kb,ab->ka", v.astype(BF16), d, preferred_element_type=F32).astype(BF16)

    def solve_t(v, d):
        return jnp.einsum("ka,ab->kb", v.astype(BF16), d, preferred_element_type=F32).astype(BF16)

    zero = jnp.zeros((half, width), BF16)
    f_par = jnp.where(level_par == 0, solve(b_par, d_par), zero)
    b_own, b_par = b_own.astype(F32), b_par.astype(F32)

    fetch = [pltpu.VMEM((width, width), BF16), pltpu.SemaphoreType.DMA]
    products = [jax.ShapeDtypeStruct((2, half, width), t) for t in (F32, BF16)]
    level_r = jnp.where(is_own, level_own, level_par)
    sums = jnp.zeros((2, half, width), F32)
    for level in range(1, LEVELS):
        f_r = jnp.where(is_own, f_own, f_par)
        sent = jnp.where(level_r == level - 1, f_r, zero)
        if level == 1:
            got = lax.all_to_all(jnp.broadcast_to(sent[None], (NZ, half, width)), "z", 0, 0)
            got = lax.dynamic_index_in_dim(got.reshape(HZ, 2, half, width), y // 2, 1, keepdims=False)
            parts = [got] + [lax.ppermute(got, "x", pairs(NX, s)) for s in (1, 2, 3)]
        else:
            got = lax.all_to_all(jnp.broadcast_to(sent[None], (NX * NZ, half, width)), ("x", "z"), 0, 0)
            parts = [lax.dynamic_index_in_dim(got.reshape(n_j, 2, half, width), y // 2, 1, keepdims=False)]
        if level == 1:
            plan, held, rest, got = pl.pallas_call(
                prepare,
                in_specs=[anywhere] * 2 + [smem] + [anywhere] * 2 + [vmem],
                out_specs=[smem, vmem, anywhere, vmem],
                out_shape=[
                    pltpu.SMEM((ROWS + 2,), jnp.int32),
                    pltpu.VMEM((HELD, width, width), BF16),
                    pltpu.HBM((2 * n_j - HELD, width, width), BF16),
                    jax.ShapeDtypeStruct((HZ, half, width), BF16),
                ],
                scratch_shapes=[
                    pltpu.SMEM(levels.shape, jnp.int32),
                    pltpu.SMEM((n_j,), jnp.int32),
                    pltpu.SemaphoreType.DMA((2 * n_j,)),
                ],
                compiler_params=params,

            )(in_hbm(levels), in_hbm(pattern_own), pattern_par, l_own, l_par, got)
            parts[0] = got
            plan = pltpu.with_memory_space_constraint(plan, pltpu.SMEM)
            held = pltpu.with_memory_space_constraint(held, pltpu.VMEM)
            rest = pltpu.with_memory_space_constraint(rest, pltpu.HBM)
        sums, rows = pl.pallas_call(
            functools.partial(forward_products, level),
            in_specs=[smem] + [vmem] * 2 + [anywhere, vmem],
            out_specs=[vmem] * 2,
            out_shape=products,
            scratch_shapes=fetch,
            compiler_params=params,
        )(plan, jnp.concatenate(parts), held, rest, sums)
        others = [lax.ppermute(rows, "y", pairs(NY, s)).astype(F32) for s in (1, 3, 2)]
        other = others[0] + others[1] + others[2]
        s_own = sums[0] + jnp.where(k == 0, other[0], other[1])
        s_par = sums[1] + jnp.where(k == 0, other[1], other[0])
        f_own = jnp.where(level_own == level, solve(b_own - s_own, d_own), f_own)
        f_par = jnp.where(level_par == level, solve(b_par - s_par, d_par), f_par)

    top = LEVELS - 1
    o_own = jnp.where(level_own == top, solve_t(f_own, d_own), zero)
    o_par = jnp.where(level_par == top, solve_t(f_par, d_par), zero)
    f_r = jnp.where(is_own, f_own, f_par)
    d_r = jnp.where(is_own, d_own, d_par)
    o_own, o_par, f_r, d_r = lax.optimization_barrier((o_own, o_par, f_r, d_r))
    r_sum = jnp.zeros((half, width), F32)
    for level in range(top - 1, -1, -1):
        sent = pl.pallas_call(
            functools.partial(backward_products, level),
            in_specs=[smem] + [vmem] * 3 + [anywhere],
            out_specs=vmem,
            out_shape=jax.ShapeDtypeStruct((NX * NZ, half, width), BF16),
            scratch_shapes=[pltpu.VMEM((n_j, half, width), F32)] + fetch,
            compiler_params=params,
        )(plan, o_own, o_par, held, rest)
        arrived = lax.all_to_all(sent, ("x", "z"), 0, 0)
        r_sum = r_sum + jnp.sum(arrived.astype(F32), axis=0)
        o_r = solve_t(f_r.astype(F32) - r_sum, d_r)
        got = jnp.stack([o_r] + [lax.ppermute(o_r, "y", pairs(NY, s)) for s in (1, 2, 3)])
        new_own = lax.dynamic_index_in_dim(got, y ^ (2 * (z % 2) + k), 0, keepdims=False)
        new_par = lax.dynamic_index_in_dim(got, y ^ (2 * (z % 2) + 1 - k), 0, keepdims=False)
        o_own = jnp.where(level_own == level, new_own, o_own)
        o_par = jnp.where(level_par == level, new_par, o_par)

    theirs = swap(jnp.stack([f_par, o_par]))
    mine = jnp.stack([f_own, o_own])
    both = jnp.concatenate([jnp.where(k == 0, mine, theirs), jnp.where(k == 0, theirs, mine)], axis=1)
    return (both[0][None], both[1][None])


def solution(mesh):
    fine = Mesh(mesh.devices.reshape(NX, NZ, NK, NY), ("x", "z", "k", "y"))
    row = ("x", "z", "k")
    return jax.shard_map(
        shards,
        mesh=fine,
        in_specs=(
            P(row, None, "y", None, None),
            P(row, None, None),
            P(row, None, None),
            P(),
            P(row, None, "y"),
        ),
        out_specs=(P(row, None, None), P(row, None, None)),
        check_vma=False,
    )
```
